32 devices in a mesh: wide: 8 (over y, x, core), narrow: 4 (over z).
Axes of the slice: x: 2, y: 2, z: 4, core: 2. Of those that a mesh axis runs over, the one named last changes fastest.
Arguments:
- diag_blocks: float32 [8, 512, 512], P('wide'), as said below
- row_panel: bfloat16 [8, 1024, 512], P('wide', 'narrow'), may hold values from -6 to 6
- col_panel: bfloat16 [8, 1024, 512], P('wide', 'narrow'), may hold values from -6 to 6
- row_tiles: int32 [8, 4], P('wide'), may hold values from 0 to 7, as said below
- col_mask: int32 [8, 4], P('wide', 'narrow'), may hold values 0 or 1
- slot_tile: int32 [8], replicated, may hold values from 0 to 7, each once
- trailing: float32 [2048, 1024], P('wide', 'narrow'), may hold values from -6 to 6
Outputs:
- schur_block: float32 [2048, 1024], P('wide', 'narrow')
The draws below stay inside these ranges and needn't reach their ends.
Inputs may be any that keep to these rules, and one draw needn't show every extreme that they name: `row_tiles`: the 4 ids of one supernode are distinct. `slot_tile`: a permutation of the row-tile ids. `diag_blocks`: each block is symmetric and positive definite, its smallest eigenvalue at least 30.
All inputs are finite; a program needn't handle non-finite values. No bound on the sum of `col_mask` on one device may be relied on, other than what follows from the above.
Results may differ from the reference program's by a relative error of at most 0.013.
Values may be sent and summed in bfloat16 or wider, within the bound.
A program may use at most 64 MiB of HBM per device.

```python
import jax
import jax.numpy as jnp
from jax import lax

SNW = 512
TILE = 256
SN_DEV = 1
NSUP = 8
ROW_TILES = 8
COL_TILES = 4


def draw_diag_blocks(key, part):
    factors = jax.random.normal(key, (NSUP, SNW, SNW), jnp.float32)
    gram = jnp.einsum('sik,sjk->sij', factors, factors, precision=lax.Precision.HIGHEST) / SNW
    gram = 0.5 * (gram + jnp.swapaxes(gram, 1, 2))
    identity = jnp.eye(SNW, dtype=jnp.float32)[None, :, :]
    return (50.0 * (gram + identity)).astype(jnp.float32)


def draw_row_tiles(key, part):
    subkeys = jax.random.split(jax.random.fold_in(key, 11), NSUP)

    def single(subkey):
        return jax.random.permutation(subkey, ROW_TILES)[:COL_TILES].astype(jnp.int32)
    return jax.vmap(single)(subkeys)


def touch_ends(result, own_key, least, high):
    dims = result.shape
    place = [jax.random.randint(jax.random.fold_in(own_key, axis), (), 0, dims[axis]) for axis in range(len(dims))]
    result = result.at[tuple(place)].set(least)
    longest = dims.index(max(dims))
    place[longest] = (place[longest] + 1) % dims[longest]
    return result.at[tuple(place)].set(high)


def level_of(key, extent, shards, smallest, largest):
    gain, own = 1.0, jax.random.fold_in(key, 6)
    for axis_at, blocks in shards:
        draws = jnp.exp(jax.random.uniform(jax.random.fold_in(own, axis_at), (blocks,), jnp.float32, smallest / len(shards), largest / len(shards)))
        gain = gain * jnp.repeat(draws, extent[axis_at] // blocks).reshape([-1 if axis == axis_at else 1 for axis in range(len(extent))])
    return gain


def gaussian(key, shape, spread, most, cuts=(), held_as=jnp.bfloat16):
    values = jax.random.normal(key, shape, jnp.float32) * spread
    if len(cuts) > 0:
        values = level_of(key, shape, cuts, -0.22, 0.18) * values
    return jnp.clip(values, min=-most, max=most).astype(held_as)


def setup_inputs(seed: int = 0) -> dict:
    key_list = jax.random.split(jax.random.key(seed), 8)
    return {
        "diag_blocks": draw_diag_blocks(jax.random.fold_in(key_list[7], 71), 0),
        "row_panel": gaussian(key_list[1], (NSUP, COL_TILES * TILE, SNW), 1.0, 6.0, ((0, 8), (1, 4))),
        "col_panel": gaussian(key_list[2], (NSUP, COL_TILES * TILE, SNW), 1.0, 6.0, ((0, 8), (1, 4))),
        "row_tiles": draw_row_tiles(jax.random.fold_in(key_list[7], 71), 0),
        "col_mask": touch_ends((jax.random.randint(key_list[4], (NSUP, COL_TILES), 0, 2) < 1).astype(jnp.int32), jax.random.fold_in(key_list[4], 1), 0, 1),
        "slot_tile": jax.random.permutation(key_list[5], ROW_TILES).astype(jnp.int32),
        "trailing": gaussian(key_list[6], (ROW_TILES * TILE, COL_TILES * TILE), 1.0, 6.0, ((0, 8), (1, 4)), jnp.float32),
    }


def solve_rows(panel, factor_low):
    solved = lax.linalg.triangular_solve(factor_low, panel.astype(jnp.float32), left_side=False, lower=True, transpose_a=True)
    return solved.astype(jnp.bfloat16)

def member(diagonal, rows_in, cols_in, tile_ids, present, slot_of):
    factor_low = jnp.linalg.cholesky(diagonal)
    left_side = solve_rows(rows_in, factor_low).astype(jnp.float32)
    right_side = solve_rows(cols_in, factor_low).astype(jnp.float32)
    right_side = right_side * jnp.repeat(present.astype(jnp.float32), TILE)[:, None]
    products = jnp.dot(left_side, right_side.T, precision=lax.Precision.HIGHEST)
    blocks = products.reshape(COL_TILES, TILE, COL_TILES * TILE)
    placed = jnp.zeros((ROW_TILES, TILE, COL_TILES * TILE), jnp.float32)
    return placed.at[slot_of[tile_ids]].add(blocks)

def reference(diag_blocks, row_panel, col_panel, row_tiles, col_mask, slot_tile, trailing):
    positions = jnp.arange(ROW_TILES, dtype=jnp.int32)
    slot_of = jnp.zeros((ROW_TILES,), jnp.int32).at[slot_tile].set(positions)
    groups = (diag_blocks.reshape(ROW_TILES, SN_DEV, SNW, SNW), row_panel.reshape(ROW_TILES, SN_DEV, COL_TILES * TILE, SNW), col_panel.reshape(ROW_TILES, SN_DEV, COL_TILES * TILE, SNW), row_tiles.reshape(ROW_TILES, SN_DEV, COL_TILES), col_mask.reshape(ROW_TILES, SN_DEV, COL_TILES))

    def group_step(running, inputs):
        diagonal, rows_in, cols_in, tile_ids, present = inputs
        partial_value = jnp.zeros((ROW_TILES, TILE, COL_TILES * TILE), jnp.float32)
        for which in range(SN_DEV):
            partial_value = partial_value + member(diagonal[which], rows_in[which], cols_in[which], tile_ids[which], present[which], slot_of)
        rounded = lax.optimization_barrier(partial_value.astype(jnp.bfloat16))
        return (running + rounded.astype(jnp.float32), None)
    start_sum = jnp.zeros((ROW_TILES, TILE, COL_TILES * TILE), jnp.float32)
    update, _ = lax.scan(group_step, start_sum, groups)
    return trailing - update.reshape(ROW_TILES * TILE, COL_TILES * TILE)
```

```python
import functools

import jax
import jax.numpy as jnp
from jax import lax
from jax.experimental import pallas as pl
from jax.experimental.pallas import tpu as pltpu
from jax.sharding import PartitionSpec as P

F32 = jnp.float32
BF16 = jnp.bfloat16
MESH = pl.DeviceIdType.MESH
LEAST = 30.0
ENOUGH = 1e-3
VMEM_LIMIT = 48 * 1024 * 1024


def mm(a, b):
    return jnp.dot(a, b, preferred_element_type=F32)


def split(a):
    high = a.astype(BF16)
    return high, (a - high.astype(F32)).astype(BF16)


def eliminate(diag_ref, panel_ref, solved_ref, low_ref, sides_ref):
    n = diag_ref.shape[0]
    low_ref[...] = diag_ref[...]
    sides_ref[...] = panel_ref[...].astype(F32).T
    lane = lax.broadcasted_iota(jnp.int32, (1, n), 1)
    place = lax.broadcasted_iota(jnp.int32, (n, 1), 0)

    def pivot(k, carry):
        row = low_ref[pl.ds(k, 1), :]
        side = sides_ref[pl.ds(k, 1), :]
        scale = 1.0 / jnp.sum(jnp.where(lane == k, row, 0.0), axis=1, keepdims=True)
        col = jnp.sum(jnp.where(lane == k, low_ref[...], 0.0), axis=1, keepdims=True)
        col = jnp.where(place == k, 0.0, col)
        row, side = row * scale, side * scale
        low_ref[...] = low_ref[...] - col * row
        sides_ref[...] = sides_ref[...] - col * side
        low_ref[pl.ds(k, 1), :] = row
        sides_ref[pl.ds(k, 1), :] = side
        return carry

    lax.fori_loop(0, n, pivot, 0)
    solved_ref[...] = sides_ref[...].T


def solve_kernel(diag_ref, panel_ref, high_ref, low_out_ref, e_ref, x_ref, y_ref, low_ref, sides_ref):
    n = diag_ref.shape[0]
    diag = diag_ref[...]
    eye = (
        lax.broadcasted_iota(jnp.int32, (n, n), 0) == lax.broadcasted_iota(jnp.int32, (n, n), 1)
    ).astype(F32)
    most = jnp.max(jnp.sum(jnp.abs(diag), axis=1))
    scale = 2.0 / (LEAST + most)
    gap = (most - LEAST) / (most + LEAST)
    e = eye - scale * diag
    gain = 2.0 / (2.0 - gap * gap)
    x_ref[...] = (gain * scale) * (eye + e)
    eb = e.astype(BF16)
    e_ref[...] = (1.0 - gain) * eye + gain * mm(eb, eb)
    gap = gap * gap * 0.5 * gain

    def newton(carry):
        gap, step = carry
        gain = 2.0 / (2.0 - gap * gap)
        eb = e_ref[...].astype(BF16)
        x = x_ref[...]
        x_ref[...] = gain * (x + mm(x.astype(BF16), eb))
        e_ref[...] = (1.0 - gain) * eye + gain * mm(eb, eb)
        return gap * gap * 0.5 * gain, step + 1

    lax.while_loop(lambda c: (c[0] > 0.15) & (c[1] < 16), newton, (gap, jnp.int32(0)))
    eb = e_ref[...].astype(BF16)
    x = x_ref[...]
    inverse = (x + mm(x.astype(BF16), eb)).astype(BF16)

    panel = panel_ref[...]
    size = jnp.sum(panel.astype(F32) ** 2)
    diag_high, diag_low = split(diag)
    y_ref[...] = mm(panel, inverse)

    def refine(carry):
        _, step = carry
        y = y_ref[...]
        y_high, y_low = split(y)
        rest = panel.astype(F32) - mm(y_high, diag_high) - mm(y_high, diag_low) - mm(y_low, diag_high)
        y_ref[...] = y + mm(rest.astype(BF16), inverse)
        return jnp.sum(rest * rest), step + 1

    def unfinished(carry):
        return jnp.logical_not(carry[0] <= ENOUGH * ENOUGH * size)

    left, _ = lax.while_loop(
        lambda c: unfinished(c) & (c[1] < 8), refine, refine((F32(0), jnp.int32(0)))
    )

    @pl.when(unfinished((left, 0)))
    def _():
        eliminate(diag_ref, panel_ref, y_ref, low_ref, sides_ref)

    high_ref[...], low_out_ref[...] = split(y_ref[...])


def solve(diag, panel):
    n, rows = diag.shape[0], panel.shape[0]
    return pl.pallas_call(
        solve_kernel,
        out_shape=[jax.ShapeDtypeStruct((rows, n), BF16)] * 2,
        in_specs=[pl.BlockSpec(memory_space=pltpu.VMEM)] * 2,
        out_specs=[pl.BlockSpec(memory_space=pltpu.VMEM)] * 2,
        scratch_shapes=[
            pltpu.VMEM((n, n), F32),
            pltpu.VMEM((n, n), F32),
            pltpu.VMEM((rows, n), F32),
            pltpu.VMEM((n, n), F32),
            pltpu.VMEM((n, rows), F32),
        ],
        compiler_params=pltpu.CompilerParams(vmem_limit_bytes=VMEM_LIMIT),
        cost_estimate=pl.CostEstimate(
            flops=100 * n * n * n, bytes_accessed=4 * n * n, transcendentals=0
        ),
    )(diag, panel)


def update_kernel(wide, narrow, tiles, *refs):
    place_ref, weight_ref, high_ref, low_ref, trailing_ref = refs[:5]
    panel_refs = refs[5 : 5 + tiles]
    out_ref, products, acc, first_send, first_recv, sends, recvs, first_sems, sems = refs[5 + tiles :]
    bits = wide.bit_length() - 1
    size = out_ref.shape[0]
    half = size // 2
    me = lax.axis_index("wide")
    own_bit = [lax.rem(lax.div(me, 1 << b), 2) for b in range(bits)]

    def partner(b):
        return me + (1 - 2 * own_bit[b]) * (1 << b)

    def slot(r):
        return sum(
            ((1 - own_bit[b]) if (r >> b) & 1 else own_bit[b]) * (1 << b) for b in range(bits)
        )

    barrier = pltpu.get_barrier_semaphore()
    for b in range(bits):
        pl.semaphore_signal(barrier, inc=1, device_id={"wide": partner(b)}, device_id_type=MESH)

    dims = (((1,), (1,)), ((), ()))
    for k in range(tiles):
        panel = panel_refs[k][...]
        products[k] = lax.dot_general(
            panel, high_ref[...], dims, preferred_element_type=F32
        ) + lax.dot_general(panel, low_ref[...], dims, preferred_element_type=F32)
    pl.semaphore_wait(barrier, bits)

    def own(r):
        p = slot(r)
        return products[place_ref[p]] * weight_ref[p]

    def first_copy(i):
        return pltpu.make_async_remote_copy(
            src_ref=first_send.at[i],
            dst_ref=first_recv.at[i],
            send_sem=first_sems.at[0, i],
            recv_sem=first_sems.at[1, i],
            device_id={"wide": partner(0)},
            device_id_type=MESH,
        )

    for i in range(wide // 2):
        first_send[i] = own(2 * i + 1).astype(BF16)
        first_copy(i).start()
    for i in range(wide // 2):
        first_copy(i).wait_recv()
        acc[i] = own(2 * i) + first_recv[i].astype(F32)

    orders = [list(range(1, bits)), list(range(bits - 1, 0, -1))]
    left = [list(range(0, wide, 2)), list(range(0, wide, 2))]
    base = [0, 0]
    for step in range(bits - 1):
        copies = []
        for h in range(2):
            b = orders[h][step]
            gone = [r for r in left[h] if (r >> b) & 1]
            left[h] = [r for r in left[h] if not (r >> b) & 1]
            at = base[h]
            count = len(gone)
            for i, r in enumerate(gone):
                sends[h, at + i] = acc[r // 2, h * half : (h + 1) * half, :].astype(BF16)
            copy = pltpu.make_async_remote_copy(
                src_ref=sends.at[h, pl.ds(at, count)],
                dst_ref=recvs.at[h, pl.ds(at, count)],
                send_sem=sems.at[0, h, step],
                recv_sem=sems.at[1, h, step],
                device_id={"wide": partner(b)},
                device_id_type=MESH,
            )
            copy.start()
            copies.append((copy, [r - (1 << b) for r in gone], at))
            base[h] = at + count
        for h in range(2):
            copy, kept, at = copies[h]
            copy.wait()
            for i, r in enumerate(kept):
                acc[r // 2, h * half : (h + 1) * half, :] += recvs[h, at + i].astype(F32)
    for i in range(wide // 2):
        first_copy(i).wait_send()
    out_ref[...] = trailing_ref[...] - acc[0]


def update(wide, narrow, place, weight, high, low, trailing, panels):
    tiles = len(panels)
    rows, cols = trailing.shape
    bits = wide.bit_length() - 1
    vmem = pl.BlockSpec(memory_space=pltpu.VMEM)
    smem = pl.BlockSpec(memory_space=pltpu.SMEM)
    return pl.pallas_call(
        functools.partial(update_kernel, wide, narrow, tiles),
        out_shape=jax.ShapeDtypeStruct((rows, cols), F32),
        in_specs=[smem, smem] + [vmem] * (3 + tiles),
        out_specs=vmem,
        scratch_shapes=[
            pltpu.VMEM((tiles, rows, cols), F32),
            pltpu.VMEM((wide // 2, rows, cols), F32),
            pltpu.VMEM((wide // 2, rows, cols), BF16),
            pltpu.VMEM((wide // 2, rows, cols), BF16),
            pltpu.VMEM((2, wide // 2, rows // 2, cols), BF16),
            pltpu.VMEM((2, wide // 2, rows // 2, cols), BF16),
            pltpu.SemaphoreType.DMA((2, wide // 2)),
            pltpu.SemaphoreType.DMA((2, 2, bits)),
        ],
        compiler_params=pltpu.CompilerParams(
            collective_id=0, has_side_effects=True, vmem_limit_bytes=VMEM_LIMIT
        ),
    )(place, weight, high, low, trailing, *panels)


def local(wide, narrow, diag_blocks, row_panel, col_panel, row_tiles, col_mask, slot_tile, trailing):
    panel = row_panel[0]
    shifted = [panel]
    for d in range(1, narrow):
        shifted.append(lax.ppermute(panel, "narrow", [(i, (i + d) % narrow) for i in range(narrow)]))
    high, low = solve(diag_blocks[0], col_panel[0])
    own = lax.axis_index("narrow")
    hits = slot_tile[:, None] == row_tiles[0][None, :]
    distance = (own - jnp.arange(narrow, dtype=jnp.int32)) % narrow
    place = jnp.sum(jnp.where(hits, distance[None, :], 0), axis=1).astype(jnp.int32)
    weight = jnp.any(hits, axis=1).astype(F32) * col_mask[0, 0].astype(F32)
    return update(wide, narrow, place, weight, high, low, trailing, shifted)


def solution(mesh):
    placed = (
        P("wide", None, None),
        P("wide", "narrow", None),
        P("wide", "narrow", None),
        P("wide", None),
        P("wide", "narrow"),
        P(),
        P("wide", "narrow"),
    )
    return jax.shard_map(
        functools.partial(local, mesh.shape["wide"], mesh.shape["narrow"]),
        mesh=mesh,
        in_specs=placed,
        out_specs=P("wide", "narrow"),
        check_vma=False,
    )
```

```python
import functools

import jax
import jax.numpy as jnp
from jax import lax
from jax.experimental import pallas as pl
from jax.experimental.pallas import tpu as pltpu
from jax.sharding import PartitionSpec as P

F32 = jnp.float32
BF16 = jnp.bfloat16
MESH = pl.DeviceIdType.MESH
LEAST = 30.0
MOST = 64.0 * LEAST
NEWTON_STEPS = 3
REFINEMENTS = 3
CHUNKS = 4
VMEM_LIMIT = 56 * 1024 * 1024


def mm(a, b):
    return jnp.dot(a, b, preferred_element_type=F32)


def split(a):
    high = a.astype(BF16)
    return high, (a - high.astype(F32)).astype(BF16)


def eliminate(diag_ref, panel_ref, solved_ref, low_ref, sides_ref):
    n = diag_ref.shape[0]
    low_ref[...] = diag_ref[...]
    sides_ref[...] = panel_ref[...].astype(F32).T
    lane = lax.broadcasted_iota(jnp.int32, (1, n), 1)
    place = lax.broadcasted_iota(jnp.int32, (n, 1), 0)

    def pivot(k, carry):
        row = low_ref[pl.ds(k, 1), :]
        side = sides_ref[pl.ds(k, 1), :]
        scale = 1.0 / jnp.sum(jnp.where(lane == k, row, 0.0), axis=1, keepdims=True)
        col = jnp.sum(jnp.where(lane == k, low_ref[...], 0.0), axis=1, keepdims=True)
        col = jnp.where(place == k, 0.0, col)
        row, side = row * scale, side * scale
        low_ref[...] = low_ref[...] - col * row
        sides_ref[...] = sides_ref[...] - col * side
        low_ref[pl.ds(k, 1), :] = row
        sides_ref[pl.ds(k, 1), :] = side
        return carry

    lax.fori_loop(0, n, pivot, 0)
    solved_ref[...] = sides_ref[...].T


def direct_kernel(diag_ref, panel_ref, flag_ref, solved_ref, low_ref, sides_ref):
    most = jnp.max(jnp.sum(jnp.abs(diag_ref[...]), axis=1))
    wide_spectrum = jnp.logical_not(most <= MOST)
    flag_ref[0] = wide_spectrum.astype(jnp.int32)

    @pl.when(wide_spectrum)
    def _():
        eliminate(diag_ref, panel_ref, solved_ref, low_ref, sides_ref)


def direct(diag, panel):
    n, rows = diag.shape[0], panel.shape[0]
    vmem = pl.BlockSpec(memory_space=pltpu.VMEM)
    return pl.pallas_call(
        direct_kernel,
        out_shape=[jax.ShapeDtypeStruct((1,), jnp.int32), jax.ShapeDtypeStruct((rows, n), F32)],
        in_specs=[vmem, vmem],
        out_specs=[pl.BlockSpec(memory_space=pltpu.SMEM), vmem],
        scratch_shapes=[pltpu.VMEM((n, n), F32), pltpu.VMEM((n, rows), F32)],
        compiler_params=pltpu.CompilerParams(vmem_limit_bytes=VMEM_LIMIT),
    )(diag, panel)


def solve(diag_ref, panel_ref, e_ref, x_ref, y_ref):
    n = diag_ref.shape[0]
    diag = diag_ref[...]
    eye = (
        lax.broadcasted_iota(jnp.int32, (n, n), 0) == lax.broadcasted_iota(jnp.int32, (n, n), 1)
    ).astype(F32)
    scale = 2.0 / (LEAST + MOST)
    gap = (MOST - LEAST) / (MOST + LEAST)
    e = eye - scale * diag
    gain = 2.0 / (2.0 - gap * gap)
    x_ref[...] = (gain * scale) * (eye + e)
    eb = e.astype(BF16)
    e_ref[...] = (1.0 - gain) * eye + gain * mm(eb, eb)
    for _ in range(NEWTON_STEPS):
        gap = gap * gap * 0.5 * gain
        gain = 2.0 / (2.0 - gap * gap)
        eb = e_ref[...].astype(BF16)
        x = x_ref[...]
        x_ref[...] = gain * (x + mm(x.astype(BF16), eb))
        e_ref[...] = (1.0 - gain) * eye + gain * mm(eb, eb)
    x = x_ref[...]
    inverse = (x + mm(x.astype(BF16), e_ref[...].astype(BF16))).astype(BF16)
    panel = panel_ref[...]
    diag_high, diag_low = split(diag)
    y_ref[...] = mm(panel, inverse)
    for _ in range(REFINEMENTS):
        y = y_ref[...]
        y_high, y_low = split(y)
        rest = panel.astype(F32) - mm(y_high, diag_high) - mm(y_high, diag_low) - mm(y_low, diag_high)
        y_ref[...] = y + mm(rest.astype(BF16), inverse)


def update_kernel(
    wide, narrow,
    place_ref, weight_ref, flag_ref, solved_ref, diag_ref, panel_ref, row_ref, trailing_ref,
    out_ref,
    e_ref, x_ref, y_ref, gathered, products, acc, sends, recvs,
    gather_send, gather_recv, wide_send, wide_recv,
):
    bits = wide.bit_length() - 1
    size = out_ref.shape[0]
    part = size // CHUNKS
    me = lax.axis_index("wide")
    pos = lax.axis_index("narrow")
    own_bit = [lax.rem(lax.div(me, 1 << b), 2) for b in range(bits)]
    has_left, has_right = pos > 0, pos < narrow - 1

    def partner(b):
        return me + (1 - 2 * own_bit[b]) * (1 << b)

    def slot(r):
        return sum(
            ((1 - own_bit[b]) if (r >> b) & 1 else own_bit[b]) * (1 << b) for b in range(bits)
        )

    barrier = pltpu.get_barrier_semaphore()
    for b in range(bits):
        pl.semaphore_signal(barrier, inc=1, device_id={"wide": partner(b)}, device_id_type=MESH)
    for there, step in ((has_left, -1), (has_right, 1)):
        @pl.when(there)
        def _(step=step):
            pl.semaphore_signal(barrier, inc=1, device_id={"narrow": pos + step}, device_id_type=MESH)
    gathered[pos] = row_ref[...]
    pl.semaphore_wait(barrier, bits + has_left.astype(jnp.int32) + has_right.astype(jnp.int32))

    def pass_on(tile, c, step):
        block = gathered.at[tile, pl.ds(c * part, part)]
        return pltpu.make_async_remote_copy(
            src_ref=block,
            dst_ref=block,
            send_sem=gather_send.at[(step + 1) // 2, tile, c],
            recv_sem=gather_recv.at[tile, c],
            device_id={"narrow": pos + step},
            device_id_type=MESH,
        )

    for c in range(CHUNKS):
        for there, step in ((has_left, -1), (has_right, 1)):
            @pl.when(there)
            def _(c=c, step=step):
                pass_on(pos, c, step).start()

    solve(diag_ref, panel_ref, e_ref, x_ref, y_ref)
    y = jnp.where(flag_ref[0] > 0, solved_ref[...], y_ref[...])
    high, low = split(y)
    dims = (((1,), (1,)), ((), ()))

    def gather(c):
        for d in range(1, narrow):
            @pl.when(pos >= d)
            def _(d=d):
                pass_on(pos - d, c, -1).wait_recv()

                @pl.when(has_right)
                def _():
                    pass_on(pos - d, c, 1).start()

            @pl.when(pos + d < narrow)
            def _(d=d):
                pass_on(pos + d, c, 1).wait_recv()

                @pl.when(has_left)
                def _():
                    pass_on(pos + d, c, -1).start()

    orders = [
        [0] + (list(range(1, bits)) if c % 2 == 0 else list(range(bits - 1, 0, -1)))
        for c in range(CHUNKS)
    ]
    left = [list(range(wide)) for _ in range(CHUNKS)]
    bases = [0] * CHUNKS
    waiting = [None] * CHUNKS

    def exchange(c, s, value):
        b = orders[c][s]
        gone = [r for r in left[c] if (r >> b) & 1]
        left[c] = [r for r in left[c] if not (r >> b) & 1]
        at, count = bases[c], len(gone)
        bases[c] = at + count
        for i, r in enumerate(gone):
            sends[c, at + i] = value(r).astype(BF16)
        copy = pltpu.make_async_remote_copy(
            src_ref=sends.at[c, pl.ds(at, count)],
            dst_ref=recvs.at[c, pl.ds(at, count)],
            send_sem=wide_send.at[c, s],
            recv_sem=wide_recv.at[c, s],
            device_id={"wide": partner(b)},
            device_id_type=MESH,
        )
        copy.start()
        waiting[c] = (copy, {r - (1 << b): at + i for i, r in enumerate(gone)})

    def multiply(c):
        rows = gathered[:, c * part : (c + 1) * part, :].reshape(narrow * part, row_ref.shape[1])
        result = lax.dot_general(rows, high, dims, preferred_element_type=F32) + lax.dot_general(
            rows, low, dims, preferred_element_type=F32
        )
        products[c] = result.reshape(narrow, part, size)
        exchange(c, 0, lambda r: own(c, r))

    def own(c, r):
        p = slot(r)
        return products[c, place_ref[p]] * weight_ref[p]

    def collect(c, s):
        copy, found = waiting[c]
        copy.wait()
        for r in left[c]:
            held = own(c, r) if s == 0 else acc[c, r]
            acc[c, r] = held + recvs[c, found[r]].astype(F32)
        if s + 1 < bits:
            exchange(c, s + 1, lambda r: acc[c, r])
        else:
            rows = slice(c * part, (c + 1) * part)
            out_ref[rows, :] = trailing_ref[rows, :] - acc[c, 0]

    for turn in range(CHUNKS + bits):
        if turn < CHUNKS:
            gather(turn)
            multiply(turn)
        for s in range(bits):
            c = turn - 1 - s
            if 0 <= c < CHUNKS:
                collect(c, s)

    for c in range(CHUNKS):
        for d in range(narrow):
            @pl.when(has_right & (pos >= d))
            def _(c=c, d=d):
                pass_on(pos - d, c, 1).wait_send()

            @pl.when(has_left & (pos + d < narrow))
            def _(c=c, d=d):
                pass_on(pos + d, c, -1).wait_send()


def update(wide, narrow, place, weight, flag, solved, diag, panel, row_panel, trailing):
    rows, cols = trailing.shape
    n = diag.shape[0]
    part = rows // CHUNKS
    bits = wide.bit_length() - 1
    vmem = pl.BlockSpec(memory_space=pltpu.VMEM)
    smem = pl.BlockSpec(memory_space=pltpu.SMEM)
    return pl.pallas_call(
        functools.partial(update_kernel, wide, narrow),
        out_shape=jax.ShapeDtypeStruct((rows, cols), F32),
        in_specs=[smem] * 3 + [vmem] * 5,
        out_specs=vmem,
        scratch_shapes=[
            pltpu.VMEM((n, n), F32),
            pltpu.VMEM((n, n), F32),
            pltpu.VMEM((panel.shape[0], n), F32),
            pltpu.VMEM((narrow,) + row_panel.shape, BF16),
            pltpu.VMEM((CHUNKS, narrow, part, cols), F32),
            pltpu.VMEM((CHUNKS, wide, part, cols), F32),
            pltpu.VMEM((CHUNKS, wide - 1, part, cols), BF16),
            pltpu.VMEM((CHUNKS, wide - 1, part, cols), BF16),
            pltpu.SemaphoreType.DMA((2, narrow, CHUNKS)),
            pltpu.SemaphoreType.DMA((narrow, CHUNKS)),
            pltpu.SemaphoreType.DMA((CHUNKS, bits)),
            pltpu.SemaphoreType.DMA((CHUNKS, bits)),
        ],
        compiler_params=pltpu.CompilerParams(
            collective_id=0, has_side_effects=True, vmem_limit_bytes=VMEM_LIMIT
        ),
    )(place, weight, flag, solved, diag, panel, row_panel, trailing)


def local(wide, narrow, diag_blocks, row_panel, col_panel, row_tiles, col_mask, slot_tile, trailing):
    flag, solved = direct(diag_blocks[0], col_panel[0])
    hits = slot_tile[:, None] == row_tiles[0][None, :]
    tile = jnp.arange(narrow, dtype=jnp.int32)
    place = jnp.sum(jnp.where(hits, tile[None, :], 0), axis=1).astype(jnp.int32)
    weight = jnp.any(hits, axis=1).astype(F32) * col_mask[0, 0].astype(F32)
    return update(
        wide, narrow, place, weight, flag, solved, diag_blocks[0], col_panel[0], row_panel[0], trailing
    )


def solution(mesh):
    placed = (
        P("wide", None, None),
        P("wide", "narrow", None),
        P("wide", "narrow", None),
        P("wide", None),
        P("wide", "narrow"),
        P(),
        P("wide", "narrow"),
    )
    return jax.shard_map(
        functools.partial(local, mesh.shape["wide"], mesh.shape["narrow"]),
        mesh=mesh,
        in_specs=placed,
        out_specs=P("wide", "narrow"),
        check_vma=False,
    )
```

```python
import functools

import jax
import jax.numpy as jnp
from jax import lax
from jax.experimental import pallas as pl
from jax.experimental.pallas import tpu as pltpu
from jax.sharding import PartitionSpec as P

F32 = jnp.float32
BF16 = jnp.bfloat16
MESH = pl.DeviceIdType.MESH
LEAST = 30.0
MOST = 64.0 * LEAST
NEWTON_STEPS = 3
REFINEMENTS = 3
CHUNKS = 4


def mm(a, b):
    return jnp.dot(a, b, preferred_element_type=F32)


def split(a):
    high = a.astype(BF16)
    return high, (a - high.astype(F32)).astype(BF16)


def eliminate(diag_ref, panel_ref, solved_ref, low_ref, sides_ref):
    n = diag_ref.shape[0]
    low_ref[...] = diag_ref[...]
    sides_ref[...] = panel_ref[...].astype(F32).T
    lane = lax.broadcasted_iota(jnp.int32, (1, n), 1)
    place = lax.broadcasted_iota(jnp.int32, (n, 1), 0)

    def pivot(k, carry):
        row = low_ref[pl.ds(k, 1), :]
        side = sides_ref[pl.ds(k, 1), :]
        scale = 1.0 / jnp.sum(jnp.where(lane == k, row, 0.0), axis=1, keepdims=True)
        col = jnp.sum(jnp.where(lane == k, low_ref[...], 0.0), axis=1, keepdims=True)
        col = jnp.where(place == k, 0.0, col)
        row, side = row * scale, side * scale
        low_ref[...] = low_ref[...] - col * row
        sides_ref[...] = sides_ref[...] - col * side
        low_ref[pl.ds(k, 1), :] = row
        sides_ref[pl.ds(k, 1), :] = side
        return carry

    lax.fori_loop(0, n, pivot, 0)
    solved_ref[...] = sides_ref[...].T


def direct_kernel(diag_ref, panel_ref, flag_ref, solved_ref, low_ref, sides_ref):
    most = jnp.max(jnp.sum(jnp.abs(diag_ref[...]), axis=1))
    wide_spectrum = jnp.logical_not(most <= MOST)
    flag_ref[0] = wide_spectrum.astype(jnp.int32)

    @pl.when(wide_spectrum)
    def _():
        eliminate(diag_ref, panel_ref, solved_ref, low_ref, sides_ref)


def direct(diag, panel):
    n, rows = diag.shape[0], panel.shape[0]
    vmem = pl.BlockSpec(memory_space=pltpu.VMEM)
    return pl.pallas_call(
        direct_kernel,
        out_shape=[jax.ShapeDtypeStruct((1,), jnp.int32), jax.ShapeDtypeStruct((rows, n), F32)],
        in_specs=[vmem, vmem],
        out_specs=[pl.BlockSpec(memory_space=pltpu.SMEM), vmem],
        scratch_shapes=[pltpu.VMEM((n, n), F32), pltpu.VMEM((n, rows), F32)],
        compiler_params=pltpu.CompilerParams(vmem_limit_bytes=16 * 1024 * 1024),
    )(diag, panel)


def solve(diag_ref, panel_ref, e_ref, x_ref, y_ref, between):
    n = diag_ref.shape[0]
    diag = diag_ref[...]
    eye = (
        lax.broadcasted_iota(jnp.int32, (n, n), 0) == lax.broadcasted_iota(jnp.int32, (n, n), 1)
    ).astype(F32)
    scale = 2.0 / (LEAST + MOST)
    gap = (MOST - LEAST) / (MOST + LEAST)
    e = eye - scale * diag
    gain = 2.0 / (2.0 - gap * gap)
    x_ref[...] = (gain * scale) * (eye + e)
    eb = e.astype(BF16)
    e_ref[...] = (1.0 - gain) * eye + gain * mm(eb, eb)
    for _ in range(NEWTON_STEPS):
        gap = gap * gap * 0.5 * gain
        gain = 2.0 / (2.0 - gap * gap)
        eb = e_ref[...].astype(BF16)
        x = x_ref[...]
        x_ref[...] = gain * (x + mm(x.astype(BF16), eb))
        e_ref[...] = (1.0 - gain) * eye + gain * mm(eb, eb)
    between(0)
    x = x_ref[...]
    inverse = (x + mm(x.astype(BF16), e_ref[...].astype(BF16))).astype(BF16)
    panel = panel_ref[...]
    diag_high, diag_low = split(diag)
    y_ref[...] = mm(panel, inverse)
    for turn in range(REFINEMENTS):
        between(turn + 1)
        y = y_ref[...]
        y_high, y_low = split(y)
        rest = panel.astype(F32) - mm(y_high, diag_high) - mm(y_high, diag_low) - mm(y_low, diag_high)
        y_ref[...] = y + mm(rest.astype(BF16), inverse)


def update_kernel(
    wide, narrow,
    row_tiles_ref, mask_ref, slot_tile_ref, flag_ref, solved_ref, diag_ref, panel_ref, row_ref, trailing_ref,
    out_ref,
    e_ref, x_ref, y_ref, gathered, products, acc, sends, recvs,
    gather_send, gather_recv, wide_send, wide_recv,
):
    bits = wide.bit_length() - 1
    size = out_ref.shape[0]
    part = size // CHUNKS
    me = lax.axis_index("wide")
    pos = lax.axis_index("narrow")
    own_bit = [lax.rem(lax.div(me, 1 << b), 2) for b in range(bits)]
    has_left, has_right = pos > 0, pos < narrow - 1

    def partner(b):
        return me + (1 - 2 * own_bit[b]) * (1 << b)

    def slot(r):
        return sum(
            ((1 - own_bit[b]) if (r >> b) & 1 else own_bit[b]) * (1 << b) for b in range(bits)
        )

    placing = []
    for r in range(wide):
        held = slot_tile_ref[slot(r)]
        tile = found = jnp.int32(0)
        for t in range(narrow):
            hit = row_tiles_ref[0, t] == held
            tile, found = jnp.where(hit, t, tile), jnp.where(hit, 1, found)
        placing.append((tile, (found * mask_ref[0, 0]).astype(F32)))

    barrier = pltpu.get_barrier_semaphore()
    for b in range(bits):
        pl.semaphore_signal(barrier, inc=1, device_id={"wide": partner(b)}, device_id_type=MESH)
    for there, step in ((has_left, -1), (has_right, 1)):
        @pl.when(there)
        def _(step=step):
            pl.semaphore_signal(barrier, inc=1, device_id={"narrow": pos + step}, device_id_type=MESH)
    gathered[pos] = row_ref[...]
    pl.semaphore_wait(barrier, bits + has_left.astype(jnp.int32) + has_right.astype(jnp.int32))

    def pass_on(tile, c, step):
        block = gathered.at[tile, pl.ds(c * part, part)]
        return pltpu.make_async_remote_copy(
            src_ref=block,
            dst_ref=block,
            send_sem=gather_send.at[(step + 1) // 2, tile, c],
            recv_sem=gather_recv.at[tile, c],
            device_id={"narrow": pos + step},
            device_id_type=MESH,
        )

    for c in range(CHUNKS):
        for there, step in ((has_left, -1), (has_right, 1)):
            @pl.when(there)
            def _(c=c, step=step):
                pass_on(pos, c, step).start()

    def gather(c, distances):
        for d in distances:
            @pl.when(pos >= d)
            def _(d=d):
                pass_on(pos - d, c, -1).wait_recv()

                @pl.when(has_right)
                def _():
                    pass_on(pos - d, c, 1).start()

            @pl.when(pos + d < narrow)
            def _(d=d):
                pass_on(pos + d, c, 1).wait_recv()

                @pl.when(has_left)
                def _():
                    pass_on(pos + d, c, -1).start()

    def near(c):
        if c < CHUNKS:
            gather(c, [1])

    solve(diag_ref, panel_ref, e_ref, x_ref, y_ref, near)
    for c in range(REFINEMENTS + 1, CHUNKS):
        near(c)
    y = jnp.where(flag_ref[0] > 0, solved_ref[...], y_ref[...])
    high, low = split(y)
    dims = (((1,), (1,)), ((), ()))

    orders = [
        [0] + (list(range(1, bits)) if c % 2 == 0 else list(range(bits - 1, 0, -1)))
        for c in range(CHUNKS)
    ]
    left = [list(range(wide)) for _ in range(CHUNKS)]
    bases = [0] * CHUNKS
    waiting = [None] * CHUNKS

    def exchange(c, s, value):
        b = orders[c][s]
        gone = [r for r in left[c] if (r >> b) & 1]
        left[c] = [r for r in left[c] if not (r >> b) & 1]
        at, count = bases[c], len(gone)
        bases[c] = at + count
        for i, r in enumerate(gone):
            sends[c, at + i] = value(r).astype(BF16)
        copy = pltpu.make_async_remote_copy(
            src_ref=sends.at[c, pl.ds(at, count)],
            dst_ref=recvs.at[c, pl.ds(at, count)],
            send_sem=wide_send.at[c, s],
            recv_sem=wide_recv.at[c, s],
            device_id={"wide": partner(b)},
            device_id_type=MESH,
        )
        copy.start()
        waiting[c] = (copy, {r - (1 << b): at + i for i, r in enumerate(gone)})

    def multiply(c):
        rows = gathered[:, c * part : (c + 1) * part, :].reshape(narrow * part, row_ref.shape[1])
        result = lax.dot_general(rows, high, dims, preferred_element_type=F32) + lax.dot_general(
            rows, low, dims, preferred_element_type=F32
        )
        products[c] = result.reshape(narrow, part, size)
        exchange(c, 0, lambda r: own(c, r))

    def own(c, r):
        tile, weight = placing[r]
        return products[c, tile] * weight

    def collect(c, s):
        copy, found = waiting[c]
        copy.wait()
        for r in left[c]:
            held = own(c, r) if s == 0 else acc[c, r]
            acc[c, r] = held + recvs[c, found[r]].astype(F32)
        if s + 1 < bits:
            exchange(c, s + 1, lambda r: acc[c, r])
        else:
            rows = slice(c * part, (c + 1) * part)
            out_ref[rows, :] = trailing_ref[rows, :] - acc[c, 0]

    for turn in range(CHUNKS + bits):
        if turn < CHUNKS:
            gather(turn, range(2, narrow))
            multiply(turn)
        for s in range(bits):
            c = turn - 1 - s
            if 0 <= c < CHUNKS:
                collect(c, s)

    for c in range(CHUNKS):
        for d in range(narrow):
            @pl.when(has_right & (pos >= d))
            def _(c=c, d=d):
                pass_on(pos - d, c, 1).wait_send()

            @pl.when(has_left & (pos + d < narrow))
            def _(c=c, d=d):
                pass_on(pos + d, c, -1).wait_send()


def update(wide, narrow, row_tiles, mask, slot_tile, flag, solved, diag, panel, row_panel, trailing):
    rows, cols = trailing.shape
    n = diag.shape[0]
    part = rows // CHUNKS
    bits = wide.bit_length() - 1
    vmem = pl.BlockSpec(memory_space=pltpu.VMEM)
    smem = pl.BlockSpec(memory_space=pltpu.SMEM)
    tile = rows * cols * 4
    scratch = (2 * n * n + panel.shape[0] * n) * 4 + narrow * row_panel.size * 2 + tile * (narrow + 2 * wide)
    return pl.pallas_call(
        functools.partial(update_kernel, wide, narrow),
        out_shape=jax.ShapeDtypeStruct((rows, cols), F32),
        in_specs=[smem] * 4 + [vmem] * 5,
        out_specs=vmem,
        scratch_shapes=[
            pltpu.VMEM((n, n), F32),
            pltpu.VMEM((n, n), F32),
            pltpu.VMEM((panel.shape[0], n), F32),
            pltpu.VMEM((narrow,) + row_panel.shape, BF16),
            pltpu.VMEM((CHUNKS, narrow, part, cols), F32),
            pltpu.VMEM((CHUNKS, wide, part, cols), F32),
            pltpu.VMEM((CHUNKS, wide - 1, part, cols), BF16),
            pltpu.VMEM((CHUNKS, wide - 1, part, cols), BF16),
            pltpu.SemaphoreType.DMA((2, narrow, CHUNKS)),
            pltpu.SemaphoreType.DMA((narrow, CHUNKS)),
            pltpu.SemaphoreType.DMA((CHUNKS, bits)),
            pltpu.SemaphoreType.DMA((CHUNKS, bits)),
        ],
        compiler_params=pltpu.CompilerParams(
            collective_id=0, has_side_effects=True, vmem_limit_bytes=scratch + 18 * 1024 * 1024
        ),
    )(row_tiles, mask, slot_tile, flag, solved, diag, panel, row_panel, trailing)


def local(wide, narrow, diag_blocks, row_panel, col_panel, row_tiles, col_mask, slot_tile, trailing):
    diag, panel = diag_blocks[0], col_panel[0]
    flag, solved = direct(diag, panel)
    return update(
        wide, narrow, row_tiles, col_mask, slot_tile, flag, solved, diag, panel, row_panel[0], trailing
    )


def solution(mesh):
    placed = (
        P("wide", None, None),
        P("wide", "narrow", None),
        P("wide", "narrow", None),
        P("wide", None),
        P("wide", "narrow"),
        P(),
        P("wide", "narrow"),
    )
    return jax.shard_map(
        functools.partial(local, mesh.shape["wide"], mesh.shape["narrow"]),
        mesh=mesh,
        in_specs=placed,
        out_specs=P("wide", "narrow"),
        check_vma=False,
    )
```
